32 devices in a mesh: dp: 8 (over z, x), mp: 4 (over y, core).
Axes of the slice: x: 2, y: 2, z: 4, core: 2. Of those that a mesh axis runs over, the one named last changes fastest.
Arguments:
- states: bfloat16 [16, 512, 1024], P('dp'), may hold values from -36 to 36
- retrieval: float32 [16], P('dp'), may hold values from -15 to 315
- pair_query: int32 [16], replicated, may hold values from 0 to 1, as said below
- positions: int32 [16, 64], P('dp'), may hold values from 0 to 511
- targets: int32 [16, 64], P('dp'), may hold values from 0 to 16383
- proj_weight: bfloat16 [3, 1024, 1024], P(None, None, 'mp'), may hold values from -0.1875 to 0.1875
- out_weight: bfloat16 [1024, 1024], P('mp'), may hold values from -0.1875 to 0.1875
- up_weight: bfloat16 [1024, 4096], P(None, 'mp'), may hold values from -0.1875 to 0.1875
- down_weight: bfloat16 [4096, 1024], P('mp'), may hold values from -0.09375 to 0.09375
- vocab_embed: bfloat16 [16384, 1024], P('mp'), may hold values from -3 to 3
Outputs:
- proj_grad: float32 [3, 1024, 1024], P(None, 'dp', 'mp')
- out_grad: float32 [1024, 1024], P('mp', 'dp')
- up_grad: float32 [1024, 4096], P('dp', 'mp')
- down_grad: float32 [4096, 1024], P('mp', 'dp')
- score_grad: float32 [16], P('dp')
The draws below stay inside these ranges and needn't reach their ends.
Inputs may be any that keep to these rules, and one draw needn't show every extreme that they name: `pair_query`: each query has 4 to 12 pairs and some query has exactly 12; pairs of one query lie anywhere.
All inputs are finite; a program needn't handle non-finite values.
Results may differ from the reference program's by a relative error of at most 0.019.
Values may be sent and summed in bfloat16 or wider, within the bound.
A program may use at most 192 MiB of HBM per device.

```python
import math
import jax
import jax.numpy as jnp
import numpy as np
from jax import lax

D = 1024
HEAD = 64
FF = 4096
VOCAB = 16384
SEQ = 512
MASKS = 64
PAIRS_DEV = 2
PAIRS = 16
QUERIES = 2
MOST_DOCS = 12


def query_ids(key):
    queries = PAIRS // 8
    spare = MOST_DOCS - 4
    extra = jnp.zeros((queries,), jnp.int32)
    slots = (queries - 1) * spare
    if slots > 0:
        remaining = PAIRS - 4 * queries - spare
        owners = jnp.arange(slots) // spare + 1
        ranks = jax.random.permutation(jax.random.fold_in(key, 11), slots)
        taken = (ranks < remaining).astype(jnp.int32)
        extra = extra.at[owners].add(taken)
    extra = extra.at[0].add(spare)
    order = jax.random.permutation(jax.random.fold_in(key, 12), queries)
    counts = 4 + extra[order]
    bounds = jnp.cumsum(counts)
    sorted_ids = jnp.sum((jnp.arange(PAIRS)[:, None] >= bounds[None, :]).astype(jnp.int32), axis=1)
    shuffle = jax.random.permutation(jax.random.fold_in(key, 13), PAIRS)
    return sorted_ids[shuffle].astype(jnp.int32)


def draw_pair_query(key, part):
    return query_ids(key)


def draw_retrieval(key, part):
    base = jnp.clip(3.0 * jax.random.normal(jax.random.fold_in(key, 21), (PAIRS,), jnp.float32), -15.0, 15.0)
    return base


def draw_states(key, part):
    noise = jnp.clip(jax.random.normal(jax.random.fold_in(key, 41), (PAIRS, SEQ, D), jnp.float32), -6.0, 6.0)
    groups = PAIRS // PAIRS_DEV
    pairing = jax.random.permutation(jax.random.fold_in(key, 42), groups)
    pair_block = jnp.arange(PAIRS) // PAIRS_DEV
    feature_block = jnp.arange(D) // (D // groups)
    boost = jnp.where(pairing[pair_block][:, None] == feature_block[None, :], 4.0, 1.0)
    values = noise * boost[:, None, :]
    return values.astype(jnp.bfloat16)


def draw_vocab_embed(key, part):
    base = jnp.clip(0.1 * jax.random.normal(jax.random.fold_in(key, 51), (VOCAB, D), jnp.float32), -0.6, 0.6)
    return base.astype(jnp.bfloat16)


def touch_ends(entries, rng, low, high):
    longest = entries.shape.index(max(entries.shape))
    spots = []
    for shift in (0, 1):
        where = [jax.random.randint(jax.random.fold_in(rng, axis), (), 0, length) for axis, length in enumerate(entries.shape)]
        where[longest] = (where[longest] + shift) % entries.shape[longest]
        spots.append(tuple(where))
    return entries.at[spots[0]].set(low).at[spots[1]].set(high)


def block_levels(stream_key, dims, pieces, smallest, largest):
    factor_of = 1.0
    for dim, shards_of in pieces:
        heights = jax.random.uniform(jax.random.fold_in(jax.random.fold_in(stream_key, 6), dim), (shards_of,), jnp.float32, smallest / len(pieces), largest / len(pieces))
        factor_of = factor_of * jnp.repeat(jnp.exp(heights), dims[dim] // shards_of).reshape((-1,) + (1,) * (len(dims) - 1 - dim))
    return factor_of


def cumulative_ranks(number_of, slope):
    loads = [(1 << 20) // math.isqrt(standing ** slope) + 1 for standing in range(1, number_of + 1)]
    scale = 1 + sum(loads) // (1 << 30)
    return np.cumsum(np.array([max(1, weight // scale) for weight in loads]))


def ranked_ids(key, extent, number_of, lean):
    grid = cumulative_ranks(number_of, lean)
    ticket = jax.random.randint(jax.random.fold_in(key, 1), extent, 0, int(grid[number_of - 1]))
    grade = jnp.searchsorted(jnp.asarray(grid, jnp.int32), ticket, side="right")
    return jax.random.permutation(jax.random.fold_in(key, 2), number_of)[grade].astype(jnp.int32)


def gaussian(rng, dims, scale, bound, cuts=(), held_as=jnp.bfloat16):
    entries = scale * jax.random.normal(rng, dims, jnp.float32)
    if cuts:
        entries = entries * block_levels(rng, dims, cuts, -0.22, 0.18)
    return jnp.clip(entries, -bound, bound).astype(held_as)


def setup_inputs(seed: int = 0) -> dict:
    seeds = jax.random.split(jax.random.key(seed), 11)
    states = draw_states(jax.random.fold_in(seeds[10], 71), 0)
    retrieval = draw_retrieval(jax.random.fold_in(seeds[10], 71), 0)
    pair_query = draw_pair_query(jax.random.fold_in(seeds[10], 71), 0)
    positions = touch_ends(jax.random.randint(seeds[3], (PAIRS, MASKS), 0, SEQ), jax.random.fold_in(seeds[3], 1), 0, SEQ - 1).astype(jnp.int32)
    targets = touch_ends(ranked_ids(seeds[4], (PAIRS, MASKS), VOCAB, 2), jax.random.fold_in(seeds[4], 3), 0, VOCAB - 1).astype(jnp.int32)
    proj_weight = gaussian(seeds[5], (3, D, D), D ** -0.5, 0.1875, ((2, 4),))
    out_weight = gaussian(seeds[6], (D, D), D ** -0.5, 0.1875, ((0, 4),))
    up_weight = gaussian(seeds[7], (D, FF), D ** -0.5, 0.1875, ((1, 4),))
    down_weight = gaussian(seeds[8], (FF, D), FF ** -0.5, 0.09375, ((0, 4),))
    vocab_embed = draw_vocab_embed(jax.random.fold_in(seeds[10], 71), 0)
    return dict(states=states, retrieval=retrieval, pair_query=pair_query, positions=positions, targets=targets, proj_weight=proj_weight, out_weight=out_weight, up_weight=up_weight, down_weight=down_weight, vocab_embed=vocab_embed)


def round_trip(value):
    return lax.optimization_barrier(value.astype(jnp.bfloat16)).astype(jnp.float32)

def matmul(left, right):
    return jnp.dot(left, right, preferred_element_type=jnp.float32)

def matmul_tn(left, right):
    return lax.dot_general(left, right, (((0,), (0,)), ((), ())), preferred_element_type=jnp.float32)

def matmul_nt(left, right):
    return lax.dot_general(left, right, (((1,), (1,)), ((), ())), preferred_element_type=jnp.float32)

def layer_norm(value):
    centre = lax.optimization_barrier(jnp.mean(value, axis=-1, keepdims=True))
    centred = value - centre
    spread = lax.optimization_barrier(jnp.mean(centred * centred, axis=-1, keepdims=True))
    return centred * lax.rsqrt(spread + 1e-05)

def norm_back(value, cotangent):
    return jax.vjp(layer_norm, value)[1](cotangent)[0]

def gelu_tanh(value):
    return jax.nn.gelu(value, approximate=True)

def gelu_back(value, cotangent):
    return jax.vjp(gelu_tanh, value)[1](cotangent)[0]

def attention(projected):
    seq_len = projected.shape[1]
    head_count = projected.shape[2] // HEAD
    parts = projected.astype(jnp.float32).reshape(3, seq_len, head_count, HEAD)
    scores = jnp.einsum('qhd,khd->hqk', parts[0], parts[1]) * HEAD ** (-0.5)
    top_value = lax.optimization_barrier(jnp.max(scores, axis=-1, keepdims=True))
    weights = jnp.exp(scores - top_value)
    probs = round_trip(weights / lax.optimization_barrier(jnp.sum(weights, axis=-1, keepdims=True)))
    context = jnp.einsum('hqk,khd->qhd', probs, parts[2])
    return context.reshape(seq_len, head_count * HEAD)

def attention_back(projected, cotangent):
    return jax.vjp(attention, projected)[1](cotangent.astype(jnp.float32))[0]

def forward(states, proj_weight, out_weight, up_weight, down_weight):
    projected = jnp.stack([matmul(states, proj_weight[part_num]) for part_num in range(3)]).astype(jnp.bfloat16)
    context = attention(projected).astype(jnp.bfloat16)
    pre_one = states.astype(jnp.float32) + matmul(context, out_weight)
    first_norm = layer_norm(pre_one).astype(jnp.bfloat16)
    inner_act = matmul(first_norm, up_weight)
    activated = gelu_tanh(inner_act).astype(jnp.bfloat16)
    pre_two = first_norm.astype(jnp.float32) + matmul(activated, down_weight)
    final_norm = layer_norm(pre_two).astype(jnp.bfloat16)
    return (projected, context, pre_one, first_norm, inner_act, activated, pre_two, final_norm)

def vocab_terms(picked, targets, vocab_embed):
    logits = matmul_nt(picked, vocab_embed)
    top_value = lax.optimization_barrier(jnp.max(logits, axis=1))
    exp_terms = jnp.exp(logits - top_value[:, None])
    denominator = lax.optimization_barrier(jnp.sum(exp_terms, axis=1))
    target_logit = jnp.take_along_axis(logits, targets[:, None], axis=1)[:, 0]
    log_prob = target_logit - top_value - jnp.log(denominator)
    return (log_prob, exp_terms / denominator[:, None])

def masked_max(values, member):
    return lax.optimization_barrier(jnp.max(jnp.where(member, values[:, None], -1e+30), axis=0))

def masked_sum(values, member, top_value):
    shifted = jnp.where(member, values[:, None] - top_value[None, :], -1e+30)
    return lax.optimization_barrier(jnp.sum(jnp.where(member, jnp.exp(shifted), 0.0), axis=0))

def query_lse(values, member):
    top_value = masked_max(values, member)
    return top_value + jnp.log(masked_sum(values, member, top_value))

def per_pair(per_query, member):
    return lax.optimization_barrier(jnp.sum(jnp.where(member, per_query[None, :], 0.0), axis=1))

def reference(states, retrieval, pair_query, positions, targets, proj_weight, out_weight, up_weight, down_weight, vocab_embed):

    def likelihood(item):
        pair_states, pair_pos, pair_tgt = item
        final_norm = forward(pair_states, proj_weight, out_weight, up_weight, down_weight)[7]
        picked = jnp.take(final_norm, pair_pos, axis=0)
        log_prob = vocab_terms(picked, pair_tgt, vocab_embed)[0]
        return jnp.sum(log_prob) / MASKS
    doc_ll = lax.map(likelihood, (states, positions, targets))
    member = pair_query[:, None] == jnp.arange(QUERIES)[None, :]
    post_values = retrieval + doc_ll
    posterior = jnp.exp(post_values - per_pair(query_lse(post_values, member), member))
    prior = jnp.exp(retrieval - per_pair(query_lse(retrieval, member), member))
    score_grad = prior - posterior

    def accumulate(carry, item):
        pair_states, pair_pos, pair_tgt, weight = item
        projected, context, pre_one, first_norm, inner_act, activated, pre_two, final_norm = forward(pair_states, proj_weight, out_weight, up_weight, down_weight)
        picked = jnp.take(final_norm, pair_pos, axis=0)
        probs = vocab_terms(picked, pair_tgt, vocab_embed)[1]
        target_hot = (pair_tgt[:, None] == jnp.arange(VOCAB)[None, :]).astype(jnp.float32)
        dlogit = (weight / MASKS * (probs - target_hot)).astype(jnp.bfloat16)
        dpicked = matmul(dlogit, vocab_embed)
        dfinal = jnp.zeros((SEQ, D), jnp.float32).at[pair_pos].add(dpicked)
        dpre_two = norm_back(pre_two, dfinal).astype(jnp.bfloat16)
        down_term = matmul_tn(activated, dpre_two)
        dinner = gelu_back(inner_act, matmul_nt(dpre_two, down_weight)).astype(jnp.bfloat16)
        up_term = matmul_tn(first_norm, dinner)
        dfirst = dpre_two.astype(jnp.float32) + matmul_nt(dinner, up_weight)
        dpre_one = norm_back(pre_one, dfirst).astype(jnp.bfloat16)
        out_term = matmul_tn(context, dpre_one)
        dcontext = matmul_nt(dpre_one, out_weight).astype(jnp.bfloat16)
        dprojected = attention_back(projected, dcontext)
        proj_term = jnp.stack([matmul_tn(pair_states, dprojected[part_num]) for part_num in range(3)])
        return ((carry[0] + proj_term, carry[1] + out_term, carry[2] + up_term, carry[3] + down_term), None)
    zeros = (jnp.zeros((3, D, D), jnp.float32), jnp.zeros((D, D), jnp.float32), jnp.zeros((D, FF), jnp.float32), jnp.zeros((FF, D), jnp.float32))
    grads = lax.scan(accumulate, zeros, (states, positions, targets, posterior))[0]
    return (grads[0], grads[1], grads[2], grads[3], score_grad)
```

```python
import jax
import jax.numpy as jnp
from jax import lax
from jax.sharding import PartitionSpec as P

HEAD = 64


def matmul(left, right):
    return jnp.dot(left, right, preferred_element_type=jnp.float32)


def matmul_tn(left, right):
    return lax.dot_general(
        left, right, (((0,), (0,)), ((), ())), preferred_element_type=jnp.float32
    )


def matmul_nt(left, right):
    return lax.dot_general(
        left, right, (((1,), (1,)), ((), ())), preferred_element_type=jnp.float32
    )


def layer_norm(value):
    centre = jnp.mean(value, axis=-1, keepdims=True)
    centred = value - centre
    spread = jnp.mean(centred * centred, axis=-1, keepdims=True)
    return centred * lax.rsqrt(spread + 1e-05)


def norm_back(value, cotangent):
    return jax.vjp(layer_norm, value)[1](cotangent)[0]


def gelu_tanh(value):
    return jax.nn.gelu(value, approximate=True)


def gelu_back(value, cotangent):
    return jax.vjp(gelu_tanh, value)[1](cotangent)[0]


def axis_bits(axis):
    return lax.axis_size(axis).bit_length() - 1


def swap(value, axis, bit):
    pairs = [(i, i ^ (1 << bit)) for i in range(lax.axis_size(axis))]
    return lax.ppermute(value, axis, pairs)


def sum_over_mp(value):
    for bit in range(axis_bits("mp")):
        sent = value.astype(jnp.bfloat16)
        value = sent.astype(jnp.float32) + swap(sent, "mp", bit).astype(jnp.float32)
    return value


def merge_totals(first, second):
    top = jnp.maximum(first[0], second[0])
    total = first[1] * jnp.exp(first[0] - top) + second[1] * jnp.exp(second[0] - top)
    return top, total


def reverse_blocks(value):
    bits = axis_bits("dp")
    rows, width = value.shape
    split = value.reshape(rows, *([2] * bits), width >> bits)
    order = (0, *range(bits, 0, -1), bits + 1)
    return split.transpose(order).reshape(rows, width)


def scatter_sum(compute, value, axis):
    index = lax.axis_index("dp")
    width = value.shape[1] // 2
    bit = index & 1
    sent = compute(lax.dynamic_slice_in_dim(value, (1 - bit) * width, width, 1))
    received = swap(sent.astype(jnp.bfloat16), "dp", 0)
    total = compute(lax.dynamic_slice_in_dim(value, bit * width, width, 1))
    total = total + received.astype(jnp.float32)
    for step in range(1, axis_bits("dp")):
        width //= 2
        bit = (index >> step) & 1
        sent = lax.dynamic_slice_in_dim(total, (1 - bit) * width, width, axis)
        received = swap(sent.astype(jnp.bfloat16), "dp", step)
        total = lax.dynamic_slice_in_dim(total, bit * width, width, axis)
        total = total + received.astype(jnp.float32)
    return total


def masked_max(values, member):
    return jnp.max(jnp.where(member, values[:, None], -1e30), axis=0)


def masked_sum(values, member, top_value):
    shifted = jnp.where(member, values[:, None] - top_value[None, :], -1e30)
    return jnp.sum(jnp.where(member, jnp.exp(shifted), 0.0), axis=0)


def per_pair(per_query, member):
    return jnp.sum(jnp.where(member, per_query[None, :], 0.0), axis=1)


def local(
    states,
    retrieval,
    pair_query,
    positions,
    targets,
    proj_weight,
    out_weight,
    up_weight,
    down_weight,
    vocab_embed,
):
    pairs_dev, seq_len, model_width = states.shape
    mask_count = positions.shape[1]
    slots = pairs_dev * mask_count
    heads = proj_weight.shape[2] // HEAD
    flat_rows = states.reshape(pairs_dev * seq_len, model_width)

    place_hot = (positions[:, :, None] == jnp.arange(seq_len)[None, None, :]).astype(jnp.bfloat16)
    picked_states = jnp.einsum(
        "pms,psd->pmd", place_hot, states, preferred_element_type=jnp.float32
    ).astype(jnp.bfloat16).reshape(slots, model_width)

    query = matmul(picked_states, proj_weight[0]).astype(jnp.bfloat16)
    query = query.reshape(pairs_dev, mask_count, heads, HEAD)
    key = matmul(flat_rows, proj_weight[1]).astype(jnp.bfloat16)
    key = key.reshape(pairs_dev, seq_len, heads, HEAD)
    val = matmul(flat_rows, proj_weight[2]).astype(jnp.bfloat16)
    val = val.reshape(pairs_dev, seq_len, heads, HEAD)
    scores = jnp.einsum(
        "pqhd,pkhd->phqk", query, key, preferred_element_type=jnp.float32
    ) * HEAD ** (-0.5)
    weights = jnp.exp(scores - jnp.max(scores, axis=-1, keepdims=True))
    soft = weights / jnp.sum(weights, axis=-1, keepdims=True)
    probs = soft.astype(jnp.bfloat16)
    context = jnp.einsum("phqk,pkhd->pqhd", probs, val, preferred_element_type=jnp.float32)
    context = context.reshape(slots, heads * HEAD).astype(jnp.bfloat16)

    pre_one = picked_states.astype(jnp.float32) + sum_over_mp(matmul(context, out_weight))
    first_norm = layer_norm(pre_one).astype(jnp.bfloat16)
    inner_act = matmul(first_norm, up_weight)
    activated = gelu_tanh(inner_act).astype(jnp.bfloat16)
    pre_two = first_norm.astype(jnp.float32) + sum_over_mp(matmul(activated, down_weight))
    picked = layer_norm(pre_two).astype(jnp.bfloat16)

    logits = matmul_nt(picked, vocab_embed)
    vocab_local = vocab_embed.shape[0]
    local_target = targets.reshape(-1) - lax.axis_index("mp") * vocab_local
    target_hot = local_target[:, None] == jnp.arange(vocab_local)[None, :]
    top_value = jnp.max(logits, axis=1)
    denominator = jnp.sum(jnp.exp(logits - top_value[:, None]), axis=1)
    target_logit = jnp.sum(jnp.where(target_hot, logits, 0.0), axis=1)
    for bit in range(axis_bits("mp")):
        other = swap(jnp.stack([top_value, denominator, target_logit]), "mp", bit)
        top_value, denominator = merge_totals((top_value, denominator), (other[0], other[1]))
        target_logit = target_logit + other[2]
    log_prob = target_logit - top_value - jnp.log(denominator)
    doc_ll = jnp.sum(log_prob.reshape(pairs_dev, mask_count), axis=1) / mask_count

    post_values = retrieval + doc_ll
    query_count = pairs_dev * lax.axis_size("dp") // 8
    local_query = lax.dynamic_slice_in_dim(
        pair_query, lax.axis_index("dp") * pairs_dev, pairs_dev, 0
    )
    member = local_query[:, None] == jnp.arange(query_count)[None, :]
    tops = jnp.stack([masked_max(post_values, member), masked_max(retrieval, member)])
    totals = jnp.stack(
        [masked_sum(post_values, member, tops[0]), masked_sum(retrieval, member, tops[1])]
    )
    for bit in range(axis_bits("dp")):
        other = swap(jnp.stack([tops, totals]), "dp", bit)
        tops, totals = merge_totals((tops, totals), (other[0], other[1]))
    lse = tops + jnp.log(totals)
    posterior = jnp.exp(post_values - per_pair(lse[0], member))
    prior = jnp.exp(retrieval - per_pair(lse[1], member))
    score_grad = prior - posterior

    vocab_probs = jnp.exp(logits - top_value[:, None]) / denominator[:, None]
    dlogit = (vocab_probs - target_hot.astype(jnp.float32)).astype(jnp.bfloat16)
    dpicked = sum_over_mp(matmul(dlogit, vocab_embed))
    dpicked = dpicked * (jnp.repeat(posterior, mask_count)[:, None] / mask_count)

    dpre_two = norm_back(pre_two, dpicked).astype(jnp.bfloat16)
    down_grad = scatter_sum(
        lambda part: matmul_tn(activated, part), reverse_blocks(dpre_two), 1
    )
    dinner = gelu_back(inner_act, matmul_nt(dpre_two, down_weight)).astype(jnp.bfloat16)
    up_grad = scatter_sum(lambda part: matmul_tn(part, dinner), reverse_blocks(first_norm), 0)
    dfirst = dpre_two.astype(jnp.float32) + sum_over_mp(matmul_nt(dinner, up_weight))
    dpre_one = norm_back(pre_one, dfirst).astype(jnp.bfloat16)
    out_grad = scatter_sum(lambda part: matmul_tn(context, part), reverse_blocks(dpre_one), 1)

    dcontext = matmul_nt(dpre_one, out_weight).astype(jnp.bfloat16)
    dcontext = dcontext.reshape(pairs_dev, mask_count, heads, HEAD)
    turned = reverse_blocks(flat_rows)
    dval = jnp.einsum("phqk,pqhd->pkhd", probs, dcontext, preferred_element_type=jnp.float32)
    dval = dval.astype(jnp.bfloat16).reshape(pairs_dev * seq_len, heads * HEAD)
    val_grad = scatter_sum(lambda part: matmul_tn(part, dval), turned, 0)
    dprobs = jnp.einsum("pqhd,pkhd->phqk", dcontext, val, preferred_element_type=jnp.float32)
    dscores = soft * (dprobs - jnp.sum(soft * dprobs, axis=-1, keepdims=True))
    dscores = (dscores * HEAD ** (-0.5)).astype(jnp.bfloat16)
    dkey = jnp.einsum("phqk,pqhd->pkhd", dscores, query, preferred_element_type=jnp.float32)
    dkey = dkey.astype(jnp.bfloat16).reshape(pairs_dev * seq_len, heads * HEAD)
    key_grad = scatter_sum(lambda part: matmul_tn(part, dkey), turned, 0)
    dquery = jnp.einsum("phqk,pkhd->pqhd", dscores, key, preferred_element_type=jnp.float32)
    dquery = dquery.astype(jnp.bfloat16).reshape(slots, heads * HEAD)
    query_grad = scatter_sum(
        lambda part: matmul_tn(part, dquery), reverse_blocks(picked_states), 0
    )
    proj_grad = jnp.stack([query_grad, key_grad, val_grad])
    return (proj_grad, out_grad, up_grad, down_grad, score_grad)


def solution(mesh):
    return jax.shard_map(
        local,
        mesh=mesh,
        in_specs=(
            P("dp", None, None),
            P("dp"),
            P(),
            P("dp", None),
            P("dp", None),
            P(None, None, "mp"),
            P("mp", None),
            P(None, "mp"),
            P("mp", None),
            P("mp", None),
        ),
        out_specs=(P(None, "dp", "mp"), P("mp", "dp"), P("dp", "mp"), P("mp", "dp"), P("dp")),
        check_vma=False,
    )
```

```python
import jax
import jax.numpy as jnp
from jax import lax
from jax.sharding import PartitionSpec as P

HEAD = 64


def matmul(left, right):
    return jnp.dot(left, right, preferred_element_type=jnp.float32)


def matmul_tn(left, right):
    return lax.dot_general(
        left, right, (((0,), (0,)), ((), ())), preferred_element_type=jnp.float32
    )


def matmul_nt(left, right):
    return lax.dot_general(
        left, right, (((1,), (1,)), ((), ())), preferred_element_type=jnp.float32
    )


def layer_norm(value):
    centre = jnp.mean(value, axis=-1, keepdims=True)
    centred = value - centre
    spread = jnp.mean(centred * centred, axis=-1, keepdims=True)
    return centred * lax.rsqrt(spread + 1e-05)


def norm_back(value, cotangent):
    return jax.vjp(layer_norm, value)[1](cotangent)[0]


def gelu_tanh(value):
    return jax.nn.gelu(value, approximate=True)


def gelu_back(value, cotangent):
    return jax.vjp(gelu_tanh, value)[1](cotangent)[0]


def axis_bits(axis):
    return lax.axis_size(axis).bit_length() - 1


def swap(value, axis, bit):
    pairs = [(i, i ^ (1 << bit)) for i in range(lax.axis_size(axis))]
    return lax.ppermute(value, axis, pairs)


def sum_over_mp(value):
    for bit in range(axis_bits("mp")):
        sent = value.astype(jnp.bfloat16)
        value = sent.astype(jnp.float32) + swap(sent, "mp", bit).astype(jnp.float32)
    return value


def merge_totals(first, second):
    top = jnp.maximum(first[0], second[0])
    total = first[1] * jnp.exp(first[0] - top) + second[1] * jnp.exp(second[0] - top)
    return top, total


def reverse_blocks(value):
    order = [0]
    for _ in range(axis_bits("dp")):
        order = [2 * place for place in order] + [2 * place + 1 for place in order]
    width = value.shape[1] // len(order)
    return jnp.concatenate(
        [value[:, place * width : (place + 1) * width] for place in order], axis=1
    )


def scatter_sum(left, right):
    index = lax.axis_index("dp")
    width = left.shape[1] // 2
    bit = index & 1
    sent = matmul_tn(lax.dynamic_slice_in_dim(left, (1 - bit) * width, width, 1), right)
    received = swap(sent.astype(jnp.bfloat16), "dp", 0)
    total = matmul_tn(lax.dynamic_slice_in_dim(left, bit * width, width, 1), right)
    total = total + received.astype(jnp.float32)
    for step in range(1, axis_bits("dp")):
        width //= 2
        bit = (index >> step) & 1
        sent = lax.dynamic_slice_in_dim(total, (1 - bit) * width, width, 0)
        received = swap(sent.astype(jnp.bfloat16), "dp", step)
        total = lax.dynamic_slice_in_dim(total, bit * width, width, 0)
        total = total + received.astype(jnp.float32)
    return total


def gather_rows(value):
    for step in reversed(range(axis_bits("dp"))):
        value = jnp.concatenate([value, swap(value, "dp", step)], axis=0)
    return value


def gather_columns(value):
    index = lax.axis_index("dp")
    width = value.shape[-1]
    for step in reversed(range(axis_bits("dp"))):
        width //= 2
        bit = (index >> step) & 1
        sent = lax.dynamic_slice_in_dim(value, (1 - bit) * width, width, value.ndim - 1)
        kept = lax.dynamic_slice_in_dim(value, bit * width, width, value.ndim - 1)
        value = jnp.concatenate([kept, swap(sent, "dp", step)], axis=-2)
    return value


def cut_heads(value, pairs):
    rows = value.shape[0] // pairs
    groups = value.shape[1] // (2 * HEAD)
    return jnp.stack(
        [
            value[p * rows : (p + 1) * rows, g * 2 * HEAD : (g + 1) * 2 * HEAD]
            for p in range(pairs)
            for g in range(groups)
        ]
    )


def join_heads(value, pairs):
    groups = value.shape[0] // pairs
    return jnp.concatenate(
        [
            jnp.concatenate([value[p * groups + g] for g in range(groups)], axis=1)
            for p in range(pairs)
        ],
        axis=0,
    )


def own_head():
    lane = jnp.arange(2 * HEAD)[None, None, :] // HEAD
    return lane == 0, lane == 1


def spread_heads(value):
    first, second = own_head()
    return jnp.concatenate([jnp.where(first, value, 0), jnp.where(second, value, 0)], axis=1)


def fold_heads(value):
    rows = value.shape[1] // 2
    return jnp.where(own_head()[0], value[:, :rows], value[:, rows:])


def batch_nn(left, right):
    return jnp.einsum("bij,bjk->bik", left, right, preferred_element_type=jnp.float32)


def batch_nt(left, right):
    return jnp.einsum("bij,bkj->bik", left, right, preferred_element_type=jnp.float32)


def batch_tn(left, right):
    return jnp.einsum("bji,bjk->bik", left, right, preferred_element_type=jnp.float32)


def masked_max(values, member):
    return jnp.max(jnp.where(member, values[:, None], -1e30), axis=0)


def masked_sum(values, member, top_value):
    shifted = jnp.where(member, values[:, None] - top_value[None, :], -1e30)
    return jnp.sum(jnp.where(member, jnp.exp(shifted), 0.0), axis=0)


def per_pair(per_query, member):
    return jnp.sum(jnp.where(member, per_query[None, :], 0.0), axis=1)


def local(
    states,
    retrieval,
    pair_query,
    positions,
    targets,
    proj_weight,
    out_weight,
    up_weight,
    down_weight,
    vocab_embed,
):
    pairs_dev, seq_len, model_width = states.shape
    mask_count = positions.shape[1]
    slots = pairs_dev * mask_count
    head_width = proj_weight.shape[2]
    flat_rows = states.reshape(pairs_dev * seq_len, model_width)

    place_hot = (positions[:, :, None] == jnp.arange(seq_len)[None, None, :]).astype(jnp.bfloat16)
    picked_states = jnp.einsum(
        "pms,psd->pmd", place_hot, states, preferred_element_type=jnp.float32
    ).astype(jnp.bfloat16).reshape(slots, model_width)

    query = matmul(picked_states, proj_weight[0]).astype(jnp.bfloat16)
    key = cut_heads(matmul(flat_rows, proj_weight[1]).astype(jnp.bfloat16), pairs_dev)
    val = cut_heads(matmul(flat_rows, proj_weight[2]).astype(jnp.bfloat16), pairs_dev)
    query = spread_heads(cut_heads(query, pairs_dev))
    scores = batch_nt(query, key) * HEAD ** (-0.5)
    weights = jnp.exp(scores - jnp.max(scores, axis=-1, keepdims=True))
    soft = weights / jnp.sum(weights, axis=-1, keepdims=True)
    probs = soft.astype(jnp.bfloat16)
    context = fold_heads(batch_nn(probs, val)).astype(jnp.bfloat16)
    context = join_heads(context, pairs_dev)

    pre_one = picked_states.astype(jnp.float32) + sum_over_mp(matmul(context, out_weight))
    first_norm = layer_norm(pre_one).astype(jnp.bfloat16)
    inner_act = matmul(first_norm, up_weight)
    activated = gelu_tanh(inner_act).astype(jnp.bfloat16)
    lefts = gather_rows(jnp.concatenate([activated, context], axis=1))
    rights = gather_columns(jnp.stack([first_norm, picked_states]))
    pre_two = first_norm.astype(jnp.float32) + sum_over_mp(matmul(activated, down_weight))
    picked = layer_norm(pre_two).astype(jnp.bfloat16)

    logits = matmul_nt(picked, vocab_embed)
    vocab_local = vocab_embed.shape[0]
    local_target = targets.reshape(-1) - lax.axis_index("mp") * vocab_local
    target_hot = local_target[:, None] == jnp.arange(vocab_local)[None, :]
    top_value = jnp.max(logits, axis=1)
    denominator = jnp.sum(jnp.exp(logits - top_value[:, None]), axis=1)
    target_logit = jnp.sum(jnp.where(target_hot, logits, 0.0), axis=1)
    for bit in range(axis_bits("mp")):
        other = swap(jnp.stack([top_value, denominator, target_logit]), "mp", bit)
        top_value, denominator = merge_totals((top_value, denominator), (other[0], other[1]))
        target_logit = target_logit + other[2]
    log_prob = target_logit - top_value - jnp.log(denominator)
    doc_ll = jnp.sum(log_prob.reshape(pairs_dev, mask_count), axis=1) / mask_count

    post_values = retrieval + doc_ll
    query_count = pairs_dev * lax.axis_size("dp") // 8
    local_query = lax.dynamic_slice_in_dim(
        pair_query, lax.axis_index("dp") * pairs_dev, pairs_dev, 0
    )
    member = local_query[:, None] == jnp.arange(query_count)[None, :]
    tops = jnp.stack([masked_max(post_values, member), masked_max(retrieval, member)])
    totals = jnp.stack(
        [masked_sum(post_values, member, tops[0]), masked_sum(retrieval, member, tops[1])]
    )
    for bit in range(axis_bits("dp")):
        other = swap(jnp.stack([tops, totals]), "dp", bit)
        tops, totals = merge_totals((tops, totals), (other[0], other[1]))
    lse = tops + jnp.log(totals)
    posterior = jnp.exp(post_values - per_pair(lse[0], member))
    prior = jnp.exp(retrieval - per_pair(lse[1], member))
    score_grad = prior - posterior

    vocab_probs = jnp.exp(logits - top_value[:, None]) / denominator[:, None]
    dlogit = (vocab_probs - target_hot.astype(jnp.float32)).astype(jnp.bfloat16)
    dpicked = sum_over_mp(matmul(dlogit, vocab_embed))
    dpicked = dpicked * (jnp.repeat(posterior, mask_count)[:, None] / mask_count)

    dpre_two = norm_back(pre_two, dpicked).astype(jnp.bfloat16)
    dinner = gelu_back(inner_act, matmul_nt(dpre_two, down_weight)).astype(jnp.bfloat16)
    dinner_all = gather_rows(dinner)
    dfirst = dpre_two.astype(jnp.float32) + sum_over_mp(matmul_nt(dinner, up_weight))
    dpre_one = norm_back(pre_one, dfirst).astype(jnp.bfloat16)
    dpre = gather_columns(jnp.stack([dpre_two, dpre_one]))

    dcontext = matmul_nt(dpre_one, out_weight).astype(jnp.bfloat16)
    dcontext = spread_heads(cut_heads(dcontext, pairs_dev))
    dval = batch_tn(probs, dcontext).astype(jnp.bfloat16)
    dprobs = batch_nt(dcontext, val)
    dscores = soft * (dprobs - jnp.sum(soft * dprobs, axis=-1, keepdims=True))
    dscores = (dscores * HEAD ** (-0.5)).astype(jnp.bfloat16)
    dkey = batch_tn(dscores, query).astype(jnp.bfloat16)
    dquery = join_heads(fold_heads(batch_nn(dscores, key)).astype(jnp.bfloat16), pairs_dev)
    dquery_all = gather_rows(dquery)
    dkey_val = jnp.concatenate([join_heads(dkey, pairs_dev), join_heads(dval, pairs_dev)], axis=1)
    key_val_grad = scatter_sum(reverse_blocks(flat_rows), dkey_val)

    ff_width = activated.shape[1]
    down_grad = matmul_tn(lefts[:, :ff_width], dpre[0])
    out_grad = matmul_tn(lefts[:, ff_width:], dpre[1])
    up_grad = matmul_tn(rights[0], dinner_all)
    query_grad = matmul_tn(rights[1], dquery_all)
    proj_grad = jnp.stack(
        [query_grad, key_val_grad[:, :head_width], key_val_grad[:, head_width:]]
    )
    return (proj_grad, out_grad, up_grad, down_grad, score_grad)


def solution(mesh):
    return jax.shard_map(
        local,
        mesh=mesh,
        in_specs=(
            P("dp", None, None),
            P("dp"),
            P(),
            P("dp", None),
            P("dp", None),
            P(None, None, "mp"),
            P("mp", None),
            P(None, "mp"),
            P("mp", None),
            P("mp", None),
        ),
        out_specs=(P(None, "dp", "mp"), P("mp", "dp"), P("dp", "mp"), P("mp", "dp"), P("dp")),
        check_vma=False,
    )
```

```python
import jax
import jax.numpy as jnp
from jax import lax
from jax.sharding import PartitionSpec as P

HEAD = 64


def matmul(left, right):
    return jnp.dot(left, right, preferred_element_type=jnp.float32)


def matmul_tn(left, right):
    return lax.dot_general(
        left, right, (((0,), (0,)), ((), ())), preferred_element_type=jnp.float32
    )


def matmul_nt(left, right):
    return lax.dot_general(
        left, right, (((1,), (1,)), ((), ())), preferred_element_type=jnp.float32
    )


def layer_norm(value):
    centre = jnp.mean(value, axis=-1, keepdims=True)
    centred = value - centre
    spread = jnp.mean(centred * centred, axis=-1, keepdims=True)
    return centred * lax.rsqrt(spread + 1e-05)


def norm_back(value, cotangent):
    return jax.vjp(layer_norm, value)[1](cotangent)[0]


def gelu_tanh(value):
    return jax.nn.gelu(value, approximate=True)


def gelu_back(value, cotangent):
    return jax.vjp(gelu_tanh, value)[1](cotangent)[0]


def axis_bits(axis):
    return lax.axis_size(axis).bit_length() - 1


def swap(value, axis, bit):
    pairs = [(i, i ^ (1 << bit)) for i in range(lax.axis_size(axis))]
    return lax.ppermute(value, axis, pairs)


def sum_over_mp(value):
    for bit in range(axis_bits("mp")):
        sent = value.astype(jnp.bfloat16)
        value = sent.astype(jnp.float32) + swap(sent, "mp", bit).astype(jnp.float32)
    return value


def merge_lse(first, second):
    top = jnp.maximum(first, second)
    return top + jnp.log(jnp.exp(first - top) + jnp.exp(second - top))


def reverse_blocks(value):
    order = [0]
    for _ in range(axis_bits("dp")):
        order = [2 * place for place in order] + [2 * place + 1 for place in order]
    width = value.shape[1] // len(order)
    return jnp.concatenate(
        [value[:, place * width : (place + 1) * width] for place in order], axis=1
    )


def scatter_sum(left, right):
    index = lax.axis_index("dp")
    width = left.shape[1] // 2
    bit = index & 1
    sent = matmul_tn(lax.dynamic_slice_in_dim(left, (1 - bit) * width, width, 1), right)
    received = swap(sent.astype(jnp.bfloat16), "dp", 0)
    total = matmul_tn(lax.dynamic_slice_in_dim(left, bit * width, width, 1), right)
    total = total + received.astype(jnp.float32)
    for step in range(1, axis_bits("dp")):
        width //= 2
        bit = (index >> step) & 1
        sent = lax.dynamic_slice_in_dim(total, (1 - bit) * width, width, 0)
        received = swap(sent.astype(jnp.bfloat16), "dp", step)
        total = lax.dynamic_slice_in_dim(total, bit * width, width, 0)
        total = total + received.astype(jnp.float32)
    return total


def gather_rows(value, later=()):
    for turn, step in enumerate(reversed(range(axis_bits("dp")))):
        received = swap(value, "dp", step)
        if turn < len(later):
            value, received, _ = lax.optimization_barrier((value, received, later[turn]))
        value = jnp.concatenate([value, received], axis=0)
    return value


def gather_columns(value, later=()):
    index = lax.axis_index("dp")
    width = value.shape[-1]
    for turn, step in enumerate(reversed(range(axis_bits("dp")))):
        width //= 2
        bit = (index >> step) & 1
        sent = lax.dynamic_slice_in_dim(value, (1 - bit) * width, width, value.ndim - 1)
        kept = lax.dynamic_slice_in_dim(value, bit * width, width, value.ndim - 1)
        received = swap(sent, "dp", step)
        if turn < len(later):
            kept, received, _ = lax.optimization_barrier((kept, received, later[turn]))
        value = jnp.concatenate([kept, received], axis=-2)
    return value


def cut_heads(value, pairs):
    rows = value.shape[0] // pairs
    groups = value.shape[1] // (2 * HEAD)
    return jnp.stack(
        [
            value[p * rows : (p + 1) * rows, g * 2 * HEAD : (g + 1) * 2 * HEAD]
            for p in range(pairs)
            for g in range(groups)
        ]
    )


def join_heads(value, pairs):
    groups = value.shape[0] // pairs
    return jnp.concatenate(
        [
            jnp.concatenate([value[p * groups + g] for g in range(groups)], axis=1)
            for p in range(pairs)
        ],
        axis=0,
    )


def own_head():
    lane = jnp.arange(2 * HEAD)[None, None, :] // HEAD
    return lane == 0, lane == 1


def spread_heads(value):
    first, second = own_head()
    return jnp.concatenate([jnp.where(first, value, 0), jnp.where(second, value, 0)], axis=1)


def fold_heads(value):
    rows = value.shape[1] // 2
    return jnp.where(own_head()[0], value[:, :rows], value[:, rows:])


def batch_nn(left, right):
    return jnp.einsum("bij,bjk->bik", left, right, preferred_element_type=jnp.float32)


def batch_nt(left, right):
    return jnp.einsum("bij,bkj->bik", left, right, preferred_element_type=jnp.float32)


def batch_tn(left, right):
    return jnp.einsum("bji,bjk->bik", left, right, preferred_element_type=jnp.float32)


def per_pair(per_query, member):
    return jnp.sum(jnp.where(member, per_query[None, :], 0.0), axis=1)


def local(
    states,
    retrieval,
    pair_query,
    positions,
    targets,
    proj_weight,
    out_weight,
    up_weight,
    down_weight,
    vocab_embed,
):
    pairs_dev, seq_len, model_width = states.shape
    mask_count = positions.shape[1]
    slots = pairs_dev * mask_count
    head_width = proj_weight.shape[2]
    flat_rows = states.reshape(pairs_dev * seq_len, model_width)

    place_hot = (positions[:, :, None] == jnp.arange(seq_len)[None, None, :]).astype(jnp.bfloat16)
    picked_states = jnp.einsum(
        "pms,psd->pmd", place_hot, states, preferred_element_type=jnp.float32
    ).astype(jnp.bfloat16).reshape(slots, model_width)

    query = matmul(picked_states, proj_weight[0]).astype(jnp.bfloat16)
    key = cut_heads(matmul(flat_rows, proj_weight[1]).astype(jnp.bfloat16), pairs_dev)
    val = cut_heads(matmul(flat_rows, proj_weight[2]).astype(jnp.bfloat16), pairs_dev)
    query = spread_heads(cut_heads(query, pairs_dev))
    scores = batch_nt(query, key) * HEAD ** (-0.5)
    weights = jnp.exp(scores - jnp.max(scores, axis=-1, keepdims=True))
    soft = weights / jnp.sum(weights, axis=-1, keepdims=True)
    probs = soft.astype(jnp.bfloat16)
    context = fold_heads(batch_nn(probs, val)).astype(jnp.bfloat16)
    context = join_heads(context, pairs_dev)

    pre_one = picked_states.astype(jnp.float32) + sum_over_mp(matmul(context, out_weight))
    first_norm = layer_norm(pre_one).astype(jnp.bfloat16)
    inner_act = matmul(first_norm, up_weight)
    activated = gelu_tanh(inner_act).astype(jnp.bfloat16)
    pre_two = first_norm.astype(jnp.float32) + sum_over_mp(matmul(activated, down_weight))
    picked = layer_norm(pre_two).astype(jnp.bfloat16)

    logits = matmul_nt(picked, vocab_embed)
    vocab_local = vocab_embed.shape[0]
    local_target = targets.reshape(-1) - lax.axis_index("mp") * vocab_local
    target_hot = local_target[:, None] == jnp.arange(vocab_local)[None, :]
    top_value = jnp.max(logits, axis=1)
    denominator = jnp.sum(jnp.exp(logits - top_value[:, None]), axis=1)
    target_logit = jnp.sum(jnp.where(target_hot, logits, 0.0), axis=1)
    stats = jnp.stack([top_value + jnp.log(denominator), target_logit])
    is_lse = jnp.arange(2)[:, None] == 0
    for bit in range(axis_bits("mp")):
        other = swap(stats, "mp", bit)
        stats = jnp.where(is_lse, merge_lse(stats, other), stats + other)
    row_lse = stats[0]
    log_prob = stats[1] - row_lse

    later = (picked, row_lse)
    lefts = gather_rows(jnp.concatenate([activated, context], axis=1), later)
    rights = gather_columns(jnp.stack([first_norm, picked_states]), later)
    doc_ll = jnp.sum(log_prob.reshape(pairs_dev, mask_count), axis=1) / mask_count

    post_values = retrieval + doc_ll
    query_count = pairs_dev * lax.axis_size("dp") // 8
    local_query = lax.dynamic_slice_in_dim(
        pair_query, lax.axis_index("dp") * pairs_dev, pairs_dev, 0
    )
    member = local_query[:, None] == jnp.arange(query_count)[None, :]
    scored = jnp.stack([post_values, retrieval])[:, :, None]
    tops = jnp.max(jnp.where(member[None], scored, -1e30), axis=1)
    shifted = jnp.where(member[None], scored - tops[:, None, :], -1e30)
    totals = jnp.sum(jnp.where(member[None], jnp.exp(shifted), 0.0), axis=1)
    present = jnp.any(member, axis=0)[None]
    lse = jnp.where(present, tops + jnp.log(jnp.where(present, totals, 1.0)), -1e30)
    for bit in range(axis_bits("dp")):
        lse = merge_lse(lse, swap(lse, "dp", bit))
    posterior = jnp.exp(post_values - per_pair(lse[0], member))
    prior = jnp.exp(retrieval - per_pair(lse[1], member))
    score_grad = prior - posterior

    vocab_probs = jnp.exp(logits - row_lse[:, None])
    dlogit = (vocab_probs - target_hot.astype(jnp.float32)).astype(jnp.bfloat16)
    dpicked = sum_over_mp(matmul(dlogit, vocab_embed))
    dpicked = dpicked * (jnp.repeat(posterior, mask_count)[:, None] / mask_count)

    dpre_two = norm_back(pre_two, dpicked).astype(jnp.bfloat16)
    dinner = gelu_back(inner_act, matmul_nt(dpre_two, down_weight)).astype(jnp.bfloat16)
    dfirst = dpre_two.astype(jnp.float32) + sum_over_mp(matmul_nt(dinner, up_weight))
    dpre_one = norm_back(pre_one, dfirst).astype(jnp.bfloat16)
    dinner_all = gather_rows(dinner, (dpre_one,))
    dpre = gather_columns(jnp.stack([dpre_two, dpre_one]))

    dcontext = matmul_nt(dpre_one, out_weight).astype(jnp.bfloat16)
    dcontext = spread_heads(cut_heads(dcontext, pairs_dev))
    dval = batch_tn(probs, dcontext).astype(jnp.bfloat16)
    dprobs = batch_nt(dcontext, val)
    dscores = soft * (dprobs - jnp.sum(soft * dprobs, axis=-1, keepdims=True))
    dscores = lax.optimization_barrier((dscores * HEAD ** (-0.5)).astype(jnp.bfloat16))
    dkey = batch_tn(dscores, query).astype(jnp.bfloat16)
    dquery = join_heads(fold_heads(batch_nn(dscores, key)).astype(jnp.bfloat16), pairs_dev)
    dquery_all = gather_rows(dquery)
    dkey_val = jnp.concatenate([join_heads(dkey, pairs_dev), join_heads(dval, pairs_dev)], axis=1)
    key_val_grad = scatter_sum(reverse_blocks(flat_rows), dkey_val)

    ff_width = activated.shape[1]
    down_grad = matmul_tn(lefts[:, :ff_width], dpre[0])
    out_grad = matmul_tn(lefts[:, ff_width:], dpre[1])
    up_grad = matmul_tn(rights[0], dinner_all)
    query_grad = matmul_tn(rights[1], dquery_all)
    proj_grad = jnp.stack(
        [query_grad, key_val_grad[:, :head_width], key_val_grad[:, head_width:]]
    )
    return (proj_grad, out_grad, up_grad, down_grad, score_grad)


def solution(mesh):
    return jax.shard_map(
        local,
        mesh=mesh,
        in_specs=(
            P("dp", None, None),
            P("dp"),
            P(),
            P("dp", None),
            P("dp", None),
            P(None, None, "mp"),
            P("mp", None),
            P(None, "mp"),
            P("mp", None),
            P("mp", None),
        ),
        out_specs=(P(None, "dp", "mp"), P("mp", "dp"), P("dp", "mp"), P("mp", "dp"), P("dp")),
        check_vma=False,
    )
```

```python
import jax
import jax.numpy as jnp
from jax import lax
from jax.sharding import PartitionSpec as P

HEAD = 64


def matmul(left, right):
    return jnp.dot(left, right, preferred_element_type=jnp.float32)


def matmul_tn(left, right):
    return lax.dot_general(
        left, right, (((0,), (0,)), ((), ())), preferred_element_type=jnp.float32
    )


def matmul_nt(left, right):
    return lax.dot_general(
        left, right, (((1,), (1,)), ((), ())), preferred_element_type=jnp.float32
    )


def layer_norm(value):
    centre = jnp.mean(value, axis=-1, keepdims=True)
    centred = value - centre
    spread = jnp.mean(centred * centred, axis=-1, keepdims=True)
    return centred * lax.rsqrt(spread + 1e-05)


def norm_back(value, cotangent):
    return jax.vjp(layer_norm, value)[1](cotangent)[0]


def gelu_tanh(value):
    return jax.nn.gelu(value, approximate=True)


def gelu_back(value, cotangent):
    return jax.vjp(gelu_tanh, value)[1](cotangent)[0]


def axis_bits(axis):
    return lax.axis_size(axis).bit_length() - 1


def swap(value, axis, bit):
    pairs = [(i, i ^ (1 << bit)) for i in range(lax.axis_size(axis))]
    return lax.ppermute(value, axis, pairs)


def sum_over_mp(value):
    for bit in range(axis_bits("mp")):
        sent = value.astype(jnp.bfloat16)
        value = sent.astype(jnp.float32) + swap(sent, "mp", bit).astype(jnp.float32)
    return value


def merge_lse(first, second):
    top = jnp.maximum(first, second)
    return top + jnp.log(jnp.exp(first - top) + jnp.exp(second - top))


def reverse_blocks(value):
    order = [0]
    for _ in range(axis_bits("dp")):
        order = [2 * place for place in order] + [2 * place + 1 for place in order]
    width = value.shape[1] // len(order)
    return jnp.concatenate(
        [value[:, place * width : (place + 1) * width] for place in order], axis=1
    )


def scatter_sum(left, right):
    index = lax.axis_index("dp")
    width = left.shape[1] // 2
    bit = index & 1
    sent = matmul_tn(lax.dynamic_slice_in_dim(left, (1 - bit) * width, width, 1), right)
    received = swap(sent.astype(jnp.bfloat16), "dp", 0)
    total = matmul_tn(lax.dynamic_slice_in_dim(left, bit * width, width, 1), right)
    total = total + received.astype(jnp.float32)
    for step in range(1, axis_bits("dp")):
        width //= 2
        bit = (index >> step) & 1
        sent = lax.dynamic_slice_in_dim(total, (1 - bit) * width, width, 0)
        received = swap(sent.astype(jnp.bfloat16), "dp", step)
        total = lax.dynamic_slice_in_dim(total, bit * width, width, 0)
        total = total + received.astype(jnp.float32)
    return total


def gather_rows(value, later=(), first=None, last=0):
    first = axis_bits("dp") if first is None else first
    for turn, step in enumerate(reversed(range(last, first))):
        received = swap(value, "dp", step)
        if turn < len(later):
            value, received, _ = lax.optimization_barrier((value, received, later[turn]))
        value = jnp.concatenate([value, received], axis=0)
    return value


def gather_columns(value, later=()):
    index = lax.axis_index("dp")
    width = value.shape[-1]
    for turn, step in enumerate(reversed(range(axis_bits("dp")))):
        width //= 2
        bit = (index >> step) & 1
        sent = lax.dynamic_slice_in_dim(value, (1 - bit) * width, width, value.ndim - 1)
        kept = lax.dynamic_slice_in_dim(value, bit * width, width, value.ndim - 1)
        received = swap(sent, "dp", step)
        if turn < len(later):
            kept, received, _ = lax.optimization_barrier((kept, received, later[turn]))
        value = jnp.concatenate([kept, received], axis=-2)
    return value


def cut_heads(value, pairs):
    rows = value.shape[0] // pairs
    groups = value.shape[1] // (2 * HEAD)
    return jnp.stack(
        [
            value[p * rows : (p + 1) * rows, g * 2 * HEAD : (g + 1) * 2 * HEAD]
            for p in range(pairs)
            for g in range(groups)
        ]
    )


def join_heads(value, pairs):
    groups = value.shape[0] // pairs
    return jnp.concatenate(
        [
            jnp.concatenate([value[p * groups + g] for g in range(groups)], axis=1)
            for p in range(pairs)
        ],
        axis=0,
    )


def own_head():
    lane = jnp.arange(2 * HEAD)[None, None, :] // HEAD
    return lane == 0, lane == 1


def spread_heads(value):
    first, second = own_head()
    return jnp.concatenate([jnp.where(first, value, 0), jnp.where(second, value, 0)], axis=1)


def fold_heads(value):
    rows = value.shape[1] // 2
    return jnp.where(own_head()[0], value[:, :rows], value[:, rows:])


def batch_nn(left, right):
    return jnp.einsum("bij,bjk->bik", left, right, preferred_element_type=jnp.float32)


def batch_nt(left, right):
    return jnp.einsum("bij,bkj->bik", left, right, preferred_element_type=jnp.float32)


def batch_tn(left, right):
    return jnp.einsum("bji,bjk->bik", left, right, preferred_element_type=jnp.float32)


def per_pair(per_query, member):
    return jnp.sum(jnp.where(member, per_query[None, :], 0.0), axis=1)


def local(
    states,
    retrieval,
    pair_query,
    positions,
    targets,
    proj_weight,
    out_weight,
    up_weight,
    down_weight,
    vocab_embed,
):
    pairs_dev, seq_len, model_width = states.shape
    mask_count = positions.shape[1]
    slots = pairs_dev * mask_count
    head_width = proj_weight.shape[2]
    flat_rows = states.reshape(pairs_dev * seq_len, model_width)

    place_hot = (positions[:, :, None] == jnp.arange(seq_len)[None, None, :]).astype(jnp.bfloat16)
    picked_states = jnp.einsum(
        "pms,psd->pmd", place_hot, states, preferred_element_type=jnp.float32
    ).astype(jnp.bfloat16).reshape(slots, model_width)

    query = matmul(picked_states, proj_weight[0]).astype(jnp.bfloat16)
    key = cut_heads(matmul(flat_rows, proj_weight[1]).astype(jnp.bfloat16), pairs_dev)
    val = cut_heads(matmul(flat_rows, proj_weight[2]).astype(jnp.bfloat16), pairs_dev)
    query = spread_heads(cut_heads(query, pairs_dev))
    scores = batch_nt(query, key) * HEAD ** (-0.5)
    weights = jnp.exp(scores - jnp.max(scores, axis=-1, keepdims=True))
    soft = weights / jnp.sum(weights, axis=-1, keepdims=True)
    probs = soft.astype(jnp.bfloat16)
    context = fold_heads(batch_nn(probs, val)).astype(jnp.bfloat16)
    context = join_heads(context, pairs_dev)

    pre_one = picked_states.astype(jnp.float32) + sum_over_mp(matmul(context, out_weight))
    first_norm = layer_norm(pre_one).astype(jnp.bfloat16)
    inner_act = matmul(first_norm, up_weight)
    activated = gelu_tanh(inner_act).astype(jnp.bfloat16)
    pre_two = first_norm.astype(jnp.float32) + sum_over_mp(matmul(activated, down_weight))
    picked = layer_norm(pre_two).astype(jnp.bfloat16)

    logits = matmul_nt(picked, vocab_embed)
    vocab_local = vocab_embed.shape[0]
    local_target = targets.reshape(-1) - lax.axis_index("mp") * vocab_local
    target_hot = local_target[:, None] == jnp.arange(vocab_local)[None, :]
    top_value = jnp.max(logits, axis=1)
    denominator = jnp.sum(jnp.exp(logits - top_value[:, None]), axis=1)
    target_logit = jnp.sum(jnp.where(target_hot, logits, 0.0), axis=1)
    stats = jnp.stack([top_value + jnp.log(denominator), target_logit])
    is_lse = jnp.arange(2)[:, None] == 0
    for bit in range(axis_bits("mp")):
        other = swap(stats, "mp", bit)
        stats = jnp.where(is_lse, merge_lse(stats, other), stats + other)
    row_lse = stats[0]
    log_prob = stats[1] - row_lse

    later = (picked, row_lse)
    lefts = gather_rows(jnp.concatenate([activated, context], axis=1), later)
    rights = gather_columns(jnp.stack([first_norm, picked_states]), later)
    doc_ll = jnp.sum(log_prob.reshape(pairs_dev, mask_count), axis=1) / mask_count

    post_values = retrieval + doc_ll
    query_count = pairs_dev * lax.axis_size("dp") // 8
    local_query = lax.dynamic_slice_in_dim(
        pair_query, lax.axis_index("dp") * pairs_dev, pairs_dev, 0
    )
    member = local_query[:, None] == jnp.arange(query_count)[None, :]
    scored = jnp.stack([post_values, retrieval])[:, :, None]
    tops = jnp.max(jnp.where(member[None], scored, -1e30), axis=1)
    shifted = jnp.where(member[None], scored - tops[:, None, :], -1e30)
    totals = jnp.sum(jnp.where(member[None], jnp.exp(shifted), 0.0), axis=1)
    present = jnp.any(member, axis=0)[None]
    lse = jnp.where(present, tops + jnp.log(jnp.where(present, totals, 1.0)), -1e30)
    for bit in range(axis_bits("dp")):
        lse = merge_lse(lse, swap(lse, "dp", bit))
    posterior = jnp.exp(post_values - per_pair(lse[0], member))
    prior = jnp.exp(retrieval - per_pair(lse[1], member))
    score_grad = prior - posterior

    vocab_probs = jnp.exp(logits - row_lse[:, None])
    dlogit = (vocab_probs - target_hot.astype(jnp.float32)).astype(jnp.bfloat16)
    dpicked = sum_over_mp(matmul(dlogit, vocab_embed))
    dpicked = dpicked * (jnp.repeat(posterior, mask_count)[:, None] / mask_count)

    dpre_two = norm_back(pre_two, dpicked).astype(jnp.bfloat16)
    dinner = gelu_back(inner_act, matmul_nt(dpre_two, down_weight)).astype(jnp.bfloat16)
    dfirst = dpre_two.astype(jnp.float32) + sum_over_mp(matmul_nt(dinner, up_weight))
    dpre_one = norm_back(pre_one, dfirst).astype(jnp.bfloat16)
    dinner_part = gather_rows(dinner, (dpre_one,), last=1)
    dpre = gather_columns(jnp.stack([dpre_two, dpre_one]))

    dcontext = matmul_nt(dpre_one, out_weight).astype(jnp.bfloat16)
    dcontext = spread_heads(cut_heads(dcontext, pairs_dev))
    dval = batch_tn(probs, dcontext).astype(jnp.bfloat16)
    dprobs = batch_nt(dcontext, val)
    dscores = soft * (dprobs - jnp.sum(soft * dprobs, axis=-1, keepdims=True))
    dscores = lax.optimization_barrier((dscores * HEAD ** (-0.5)).astype(jnp.bfloat16))
    dkey = batch_tn(dscores, query).astype(jnp.bfloat16)
    dquery = join_heads(fold_heads(batch_nn(dscores, key)).astype(jnp.bfloat16), pairs_dev)
    dquery_all = gather_rows(dquery)
    dkey_val = jnp.concatenate([join_heads(dkey, pairs_dev), join_heads(dval, pairs_dev)], axis=1)
    dkey_val, dinner_part, lefts = lax.optimization_barrier((dkey_val, dinner_part, lefts))
    dinner_all = gather_rows(dinner_part, first=1)
    key_val_grad = scatter_sum(reverse_blocks(flat_rows), dkey_val)

    ff_width = activated.shape[1]
    down_grad = matmul_tn(lefts[:, :ff_width], dpre[0])
    out_grad = matmul_tn(lefts[:, ff_width:], dpre[1])
    up_grad = matmul_tn(rights[0], dinner_all)
    query_grad = matmul_tn(rights[1], dquery_all)
    proj_grad = jnp.stack(
        [query_grad, key_val_grad[:, :head_width], key_val_grad[:, head_width:]]
    )
    return (proj_grad, out_grad, up_grad, down_grad, score_grad)


def solution(mesh):
    return jax.shard_map(
        local,
        mesh=mesh,
        in_specs=(
            P("dp", None, None),
            P("dp"),
            P(),
            P("dp", None),
            P("dp", None),
            P(None, None, "mp"),
            P("mp", None),
            P(None, "mp"),
            P("mp", None),
            P("mp", None),
        ),
        out_specs=(P(None, "dp", "mp"), P("mp", "dp"), P("dp", "mp"), P("mp", "dp"), P("dp")),
        check_vma=False,
    )
```
